32 devices in a mesh: pipe: 2 (over y), ctx: 4 (over z), dp: 4 (over x, core).
Axes of the slice: x: 2, y: 2, z: 4, core: 2. Of those that a mesh axis runs over, the one named last changes fastest.
Arguments:
- state: bfloat16 [2, 4, 512, 1024], P('pipe', 'dp', 'ctx'), may hold values from -36 to 36
- weights: bfloat16 [2, 2, 1024, 256], P(None, 'pipe'), may hold values from -0.1875 to 0.1875
- out_grad: bfloat16 [2, 2, 4, 512, 1024], P(None, 'pipe', 'dp', 'ctx'), may hold values from -0.59765625 to 0.59765625
- start_span: int32 [2, 4], P(None, 'dp'), may hold values from 0 to 1
- block_order: int32 [8], replicated, may hold values from 0 to 7, each once
Outputs:
- state_out: bfloat16 [2, 4, 512, 1024], P('pipe', 'dp', 'ctx')
- weight_grads: float32 [2, 2, 1024, 256], P(None, 'pipe')
The draws below stay inside these ranges and needn't reach their ends.
All inputs are finite; a program needn't handle non-finite values.
Results may differ from the reference program's by a relative error of at most 0.012.
Values may be sent and summed in bfloat16 or wider, within the bound.
A program may use at most 64 MiB of HBM per device.

```python
import math
import jax
import jax.numpy as jnp
from jax import lax

HQ = 8
HD = 128
G = 1024
S_DEV = 128
TICKS = 2
SPANS = 2
SECTIONS = 2
MB = 4
SEQ = 512
HALVES = 8
N_CTX = 4


def draw_state(key, part):
    key_list = jax.random.split(key, 3)
    shape = (SECTIONS, MB, SEQ, G)
    base_values = jnp.clip(jax.random.normal(key_list[0], shape, jnp.float32), -4.0, 4.0)
    row_scales = jnp.exp(jax.random.uniform(key_list[1], (SECTIONS, MB, SEQ, 1), jnp.float32, math.log(0.3), math.log(3.0)))
    column_scales = jnp.exp(jax.random.uniform(key_list[2], (1, 1, 1, G), jnp.float32, math.log(0.3), math.log(3.0)))
    return (base_values * row_scales * column_scales).astype(jnp.bfloat16)


def place_ends(result, rng, least, largest):
    longest = result.shape.index(max(result.shape))
    spots = []
    for shift in (0, 1):
        where = [jax.random.randint(jax.random.fold_in(rng, axis), (), 0, length) for axis, length in enumerate(result.shape)]
        where[longest] = (where[longest] + shift) % result.shape[longest]
        spots.append(tuple(where))
    return result.at[spots[0]].set(least).at[spots[1]].set(largest)


def block_levels(stream_key, shape, cuts, least, largest):
    level, own = 1.0, jax.random.fold_in(stream_key, 6)
    for dim, parts in cuts:
        draws = jnp.exp(jax.random.uniform(jax.random.fold_in(own, dim), (parts,), jnp.float32, least / len(cuts), largest / len(cuts)))
        level = level * jnp.repeat(draws, shape[dim] // parts).reshape([-1 if axis == dim else 1 for axis in range(len(shape))])
    return level


def centred(own_key, shape, deviation, limit, cuts=(), kind=jnp.bfloat16):
    factor_of = block_levels(own_key, shape, cuts, -0.22, 0.18) if cuts else 1.0
    entries = jax.random.normal(own_key, shape, jnp.float32) * deviation * factor_of
    return jnp.minimum(jnp.maximum(entries, -limit), limit).astype(kind)


def setup_inputs(seed: int = 0) -> dict:
    arg_keys = jax.random.split(jax.random.key(seed), 6)
    state = draw_state(jax.random.fold_in(arg_keys[5], 71), 0)
    weights = centred(arg_keys[1], (SPANS, SECTIONS, G, 2 * HD), G ** -0.5, 0.1875, ((1, 2),))
    out_grad = centred(arg_keys[2], (TICKS, SECTIONS, MB, SEQ, G), 0.1, 0.59765625, ((1, 2), (2, 4), (3, 4)))
    start_span = place_ends(jax.random.randint(arg_keys[3], (SECTIONS, MB), 0, 2), jax.random.fold_in(arg_keys[3], 1), 0, 1).astype(jnp.int32)
    block_order = jax.random.permutation(arg_keys[4], HALVES).astype(jnp.int32)
    return {"state": state, "weights": weights, "out_grad": out_grad, "start_span": start_span, "block_order": block_order}


EPS = 1e-05

def rms_scale(values):
    return lax.rsqrt(lax.optimization_barrier(jnp.mean(values * values, axis=-1, keepdims=True)) + EPS)

def apply_layer(carried, weight, upstream, positions):
    widened = carried.astype(jnp.float32)
    normed = (widened * rms_scale(widened)).astype(jnp.bfloat16)
    split_heads = widened.reshape(SEQ, HQ, HD)
    queries = (split_heads * rms_scale(split_heads)).astype(jnp.bfloat16)
    projected = jnp.dot(normed, weight, preferred_element_type=jnp.float32)
    key_raw = projected[:, :HD]
    key_scale = rms_scale(key_raw)
    key_unit = key_raw * key_scale
    packed = jnp.concatenate([key_unit, projected[:, HD:]], axis=1).astype(jnp.bfloat16)
    key_rows = packed[:, :HD].astype(jnp.float32)
    value_rows = packed[:, HD:].astype(jnp.float32)
    query_wide = queries.astype(jnp.float32)
    grad_wide = upstream.reshape(SEQ, HQ, HD).astype(jnp.float32)
    score_scale = 1.0 / math.sqrt(HD)

    def query_block(block_index):
        first_row = block_index * S_DEV
        query_part = lax.dynamic_slice_in_dim(query_wide, first_row, S_DEV, 0)
        grad_part = lax.dynamic_slice_in_dim(grad_wide, first_row, S_DEV, 0)
        own_positions = lax.dynamic_slice_in_dim(positions, first_row, S_DEV, 0)
        causal = positions[None, :] <= own_positions[:, None]
        scores = jnp.einsum('qhd,kd->hqk', query_part, key_rows) * score_scale
        exponent = jnp.where(causal[None], jnp.exp(scores), 0.0)
        total_weight = lax.optimization_barrier(jnp.sum(exponent, axis=-1, keepdims=True))
        probs = lax.optimization_barrier((exponent / total_weight).astype(jnp.bfloat16)).astype(jnp.float32)
        attended = jnp.einsum('hqk,kd->qhd', probs, value_rows)
        row_delta = jnp.einsum('qhd,qhd->hq', grad_part, attended)
        value_grad = jnp.einsum('hqk,qhd->kd', probs, grad_part)
        prob_grad = jnp.einsum('qhd,kd->hqk', grad_part, value_rows)
        score_grad = lax.optimization_barrier((probs * (prob_grad - row_delta[..., None]) * score_scale).astype(jnp.bfloat16)).astype(jnp.float32)
        key_grad = jnp.einsum('hqk,qhd->kd', score_grad, query_part)
        term = lax.optimization_barrier(jnp.concatenate([key_grad, value_grad], axis=1).astype(jnp.bfloat16)).astype(jnp.float32)
        return (attended, term)
    attended, terms = lax.map(query_block, jnp.arange(N_CTX, dtype=jnp.int32))
    output = attended.reshape(SEQ, HQ * HD)
    updated = (widened + output * rms_scale(output)).astype(jnp.bfloat16)
    key_sums = lax.optimization_barrier(jnp.sum(terms, axis=0))
    key_delta = key_sums[:, :HD]
    key_back = key_scale * (key_delta - key_unit * lax.optimization_barrier(jnp.mean(key_delta * key_unit, axis=-1, keepdims=True)))
    grad_rows = jnp.concatenate([key_back, key_sums[:, HD:]], axis=1).astype(jnp.bfloat16)
    return (updated, jnp.dot(normed.T, grad_rows, preferred_element_type=jnp.float32))

def reference(state, weights, out_grad, start_span, block_order):
    half_len = SEQ // HALVES
    row_ids = jnp.arange(SEQ, dtype=jnp.int32)
    positions = (block_order[row_ids // half_len] * half_len + row_ids % half_len).astype(jnp.int32)
    spans = start_span
    carried = state.reshape(SECTIONS * MB, SEQ, G)
    weight_grads = jnp.zeros((SPANS, SECTIONS, G, 2 * HD), jnp.float32)
    section_ids = jnp.arange(SECTIONS, dtype=jnp.int32)
    for tick_index in range(TICKS):
        weight_items = weights[spans, section_ids[:, None]].reshape(SECTIONS * MB, G, 2 * HD)
        upstream = out_grad[tick_index].reshape(SECTIONS * MB, SEQ, G)
        updated, item_grads = lax.map(lambda triple: apply_layer(triple[0], triple[1], triple[2], positions), (carried, weight_items, upstream))
        item_grads = item_grads.reshape(SECTIONS, MB, G, 2 * HD)
        span_mask = (jnp.arange(SPANS, dtype=jnp.int32)[:, None, None] == spans[None, :, :]).astype(jnp.float32)
        weight_grads = weight_grads + lax.optimization_barrier(jnp.sum(span_mask[:, :, :, None, None] * item_grads[None], axis=2))
        updated = updated.reshape(SECTIONS, MB, SEQ, G)
        carried = jnp.roll(updated, 1, axis=0).reshape(SECTIONS * MB, SEQ, G)
        spans = jnp.concatenate([1 - spans[-1:], spans[:-1]], axis=0)
    return (carried.reshape(SECTIONS, MB, SEQ, G), weight_grads)
```

```python
import functools
import math

import jax
import jax.numpy as jnp
from jax import lax
from jax.experimental import pallas as pl
from jax.experimental.pallas import tpu as pltpu
from jax.sharding import PartitionSpec as P

EPS = 1e-05
F32 = jnp.float32
BF16 = jnp.bfloat16
MESH = pl.DeviceIdType.MESH


def dot(a, b):
    return jnp.dot(a, b, preferred_element_type=F32)


def dot_nt(a, b):
    return lax.dot_general(a, b, (((1,), (1,)), ((), ())), preferred_element_type=F32)


def steps(count, body):
    if count <= 4:
        for index in range(count):
            body(index)
    else:
        lax.fori_loop(0, count, lambda index, none: (body(index), none)[1], None)


def kernel(
    cfg,
    state_ref,
    weights_ref,
    upstream_ref,
    span_ref,
    order_ref,
    state_out,
    gathered,
    kv,
    queries,
    up_rows,
    up_cols,
    exps,
    out_cols,
    totals,
    deltas,
    key_raw,
    updated,
    arrived,
    normed_t,
    normed_in,
    terms_out,
    terms_in,
    term_own,
    grad_rows,
    slices,
    wsend,
    wrecv,
    kv_send,
    kv_recv,
    nt_send,
    nt_recv,
    kt_send,
    kt_recv,
    gr_send,
    gr_recv,
    st_send,
    st_recv,
    ws_send,
    ws_recv,
    ga_send,
    ga_recv,
    gb_send,
    gb_recv,
):
    n_pipe, n_ctx, n_dp, ticks, half_len = cfg
    rows, feat = state_ref.shape
    hd = weights_ref.shape[2] // 2
    heads = feat // hd
    stack = heads * rows
    width = min(stack, 2 * rows)
    chunks = [slice(i * width, (i + 1) * width) for i in range(stack // width)]
    per_dev = rows // half_len
    f_ctx = feat // n_ctx
    f_dp = f_ctx // n_dp
    score_scale = 1.0 / math.sqrt(hd)
    exp_scale = score_scale * math.log2(math.e)

    sec = lax.axis_index("pipe")
    me = lax.axis_index("ctx")
    lane = lax.axis_index("dp")
    behind = lax.rem(sec + n_pipe - 1, n_pipe)
    ahead = lax.rem(sec + 1, n_pipe)

    def ctx_peer(offset):
        return lax.rem(me + offset, n_ctx)

    def dp_peer(offset):
        return lax.rem(lane + offset, n_dp)

    barrier = pltpu.get_barrier_semaphore()

    def greet(axis, who):
        pl.semaphore_signal(barrier, inc=1, device_id={axis: who}, device_id_type=MESH)

    for o in range(1, n_ctx):
        greet("ctx", ctx_peer(o))
    for o in range(1, n_dp):
        greet("dp", dp_peer(o))
    greet("pipe", behind)
    greet("pipe", ahead)

    def remote(src, dst, send, recv, axis, who):
        return pltpu.make_async_remote_copy(
            src_ref=src,
            dst_ref=dst,
            send_sem=send,
            recv_sem=recv,
            device_id={axis: who},
            device_id_type=MESH,
        )

    def kv_copy(t, o, owner, to):
        return remote(
            kv.at[t, owner], kv.at[t, owner], kv_send.at[t, o], kv_recv.at[t, owner], "ctx", to
        )

    def nt_copy(t, o, frm, to):
        return remote(
            normed_t.at[t, pl.ds(pl.multiple_of(to * f_ctx, 16), f_ctx)],
            normed_in.at[t, frm],
            nt_send.at[t, o],
            nt_recv.at[t, frm],
            "ctx",
            to,
        )

    def kt_copy(t, o, frm, to):
        return remote(
            terms_out.at[t, to],
            terms_in.at[t, frm],
            kt_send.at[t, o],
            kt_recv.at[t, frm],
            "ctx",
            to,
        )

    def gr_copy(t, o, owner, to):
        return remote(
            grad_rows.at[t, owner],
            grad_rows.at[t, owner],
            gr_send.at[t, o],
            gr_recv.at[t, owner],
            "ctx",
            to,
        )

    def st_copy(t):
        dst = state_out if t == ticks - 1 else arrived.at[t]
        return remote(updated.at[t], dst, st_send.at[t], st_recv.at[t], "pipe", ahead)

    def ws_copy(o, frm, to):
        return remote(wsend.at[to], wrecv.at[frm], ws_send.at[o], ws_recv.at[frm], "dp", to)

    def ga_copy(o, owner, to):
        return remote(
            gathered.at[owner, lane],
            gathered.at[owner, lane],
            ga_send.at[o],
            ga_recv.at[owner],
            "ctx",
            to,
        )

    def gb_copy(o, c, owner, to):
        return remote(
            gathered.at[c, owner],
            gathered.at[c, owner],
            gb_send.at[o, c],
            gb_recv.at[c, owner],
            "dp",
            to,
        )

    def positions(which, shape, axis):
        row = lax.rem(lax.broadcasted_iota(jnp.int32, shape, axis), rows)
        part = row // half_len
        base = jnp.zeros(shape, jnp.int32)
        for i in range(per_dev):
            base = jnp.where(part == i, order_ref[which * per_dev + i], base)
        return base * half_len + lax.rem(row, half_len)

    own_pos = positions(me, (1, width), 1)

    def span_at(t):
        anchor = lax.rem(sec - t + n_pipe * ticks, n_pipe)
        return lax.rem(span_ref[anchor, 0] + (anchor + t) // n_pipe, 2)

    def begin(t, source):
        x = source[...].astype(F32)
        squares = x * x
        sums = [
            jnp.sum(squares[:, h * hd : (h + 1) * hd], axis=1, keepdims=True) for h in range(heads)
        ]
        scale = lax.rsqrt(sum(sums[1:], sums[0]) * (1.0 / feat) + EPS)
        normed = (x * scale).astype(BF16)
        projected = dot(normed, weights_ref[span_at(t)])
        raw = projected[:, :hd]
        key_raw[t] = raw
        key_unit = raw * lax.rsqrt(jnp.mean(raw * raw, axis=1, keepdims=True) + EPS)
        kv[t, me] = jnp.concatenate([key_unit, projected[:, hd:]], axis=1).astype(BF16)
        if t == 0:
            pl.semaphore_wait(barrier, n_ctx + n_dp)
        for o in range(1, n_ctx):
            kv_copy(t, o, me, ctx_peer(o)).start()
        for h in range(heads):
            part = x[:, h * hd : (h + 1) * hd]
            queries[h * rows : (h + 1) * rows, :] = (
                part * lax.rsqrt(sums[h] * (1.0 / hd) + EPS)
            ).astype(BF16)
            normed_t[t, h * hd : (h + 1) * hd, :] = (part * scale).T.astype(BF16)
            up = upstream_ref[t, :, h * hd : (h + 1) * hd]
            up_rows[h * rows : (h + 1) * rows, :] = up
            up_cols[:, h * rows : (h + 1) * rows] = up.astype(F32).T.astype(BF16)
        for o in range(1, n_ctx):
            nt_copy(t, o, me, ctx_peer(o)).start()

    def attend(t, block, first):
        keys = kv[t, block, :, :hd]
        values_t = kv[t, block, :, hd:].astype(F32).T.astype(BF16)
        causal = positions(block, (rows, 1), 0) <= own_pos
        for cut in chunks:
            scores = dot_nt(keys, queries[cut, :])
            weight = jnp.where(causal, jnp.exp2(scores * exp_scale), 0.0)
            total = jnp.sum(weight, axis=0, keepdims=True)
            rounded = weight.astype(BF16)
            exps[block, :, cut] = rounded
            mixed = dot(values_t, rounded)
            if first:
                totals[:, cut] = total
                out_cols[:, cut] = mixed
            else:
                totals[:, cut] += total
                out_cols[:, cut] += mixed

    def update(t, source):
        inverse = 1.0 / totals[...]
        totals[...] = inverse
        power = jnp.zeros((1, rows), F32)
        for h in range(heads):
            cut = slice(h * rows, (h + 1) * rows)
            part = out_cols[:, cut] * inverse[:, cut]
            out_cols[:, cut] = part
            deltas[:, cut] = jnp.sum(part * up_cols[:, cut].astype(F32), axis=0, keepdims=True)
            power = power + jnp.sum(part * part, axis=0, keepdims=True)
        scale = lax.rsqrt(power * (1.0 / feat) + EPS)
        for h in range(heads):
            cut = slice(h * hd, (h + 1) * hd)
            part = (out_cols[:, h * rows : (h + 1) * rows] * scale).T
            updated[t, :, cut] = (source[:, cut].astype(F32) + part).astype(BF16)
        st_copy(t).start()

    def backward(t, block):
        values = kv[t, block, :, hd:]
        key_grad = jnp.zeros((rows, hd), F32)
        value_grad = jnp.zeros((rows, hd), F32)
        for cut in chunks:
            probs = exps[block, :, cut].astype(F32) * totals[:, cut]
            prob_grad = dot(values, up_cols[:, cut])
            score_grad = (probs * (prob_grad - deltas[:, cut])).astype(BF16)
            value_grad = value_grad + dot(probs.astype(BF16), up_rows[cut, :])
            key_grad = key_grad + dot(score_grad, queries[cut, :])
        return jnp.concatenate([key_grad * score_scale, value_grad], axis=1).astype(BF16)

    def finish_rows(t):
        sums = term_own[t].astype(F32)
        for o in range(1, n_ctx):
            peer = ctx_peer(o)
            kt_copy(t, o, peer, me).wait_recv()
            sums = sums + terms_in[t, peer].astype(F32)
        raw = key_raw[t]
        scale = lax.rsqrt(jnp.mean(raw * raw, axis=1, keepdims=True) + EPS)
        unit = raw * scale
        delta = sums[:, :hd]
        back = scale * (delta - unit * jnp.mean(delta * unit, axis=1, keepdims=True))
        grad_rows[t, me] = jnp.concatenate([back, sums[:, hd:]], axis=1).astype(BF16)
        for o in range(1, n_ctx):
            gr_copy(t, o, me, ctx_peer(o)).start()

    def weight_slice(t):
        own = normed_t[t, pl.ds(pl.multiple_of(me * f_ctx, 16), f_ctx), :]
        total = dot(own, grad_rows[t, me])
        for o in range(1, n_ctx):
            peer = ctx_peer(o)
            nt_copy(t, o, peer, me).wait_recv()
            gr_copy(t, o, peer, me).wait_recv()
            total = total + dot(normed_in[t, peer], grad_rows[t, peer])
        return total

    for t in range(ticks):
        if t == 0:
            source = state_ref
        else:
            st_copy(t - 1).wait_recv()
            source = arrived.at[t - 1]
        begin(t, source)
        attend(t, me, True)
        if t > 0:
            finish_rows(t - 1)

        def later(index, t=t):
            peer = ctx_peer(index + 1)
            kv_copy(t, 0, peer, me).wait_recv()
            attend(t, peer, False)

        steps(n_ctx - 1, later)
        update(t, source)

        def give(index, t=t):
            peer = ctx_peer(index + 1)
            terms_out[t, peer] = backward(t, peer)
            kt_copy(t, index + 1, me, peer).start()

        steps(n_ctx - 1, give)
        term_own[t] = backward(t, me)

    for t in range(ticks - 1):
        slices[t] = weight_slice(t)
    finish_rows(ticks - 1)
    slices[ticks - 1] = weight_slice(ticks - 1)
    picked = [span_at(t).astype(F32) for t in range(ticks)]
    for d in range(n_dp):
        cut = slice(d * f_dp, (d + 1) * f_dp)
        parts = [slices[t, cut, :] for t in range(ticks)]
        high = sum(part * pick for part, pick in zip(parts, picked))
        low = sum(part * (1.0 - pick) for part, pick in zip(parts, picked))
        wsend[d, 0] = low.astype(BF16)
        wsend[d, 1] = high.astype(BF16)
    for o in range(1, n_dp):
        ws_copy(o, lane, dp_peer(o)).start()
    total = wsend[lane].astype(F32)
    for o in range(1, n_dp):
        peer = dp_peer(o)
        ws_copy(o, peer, lane).wait_recv()
        total = total + wrecv[peer].astype(F32)
    gathered[me, lane] = total.astype(BF16)
    for o in range(1, n_ctx):
        ga_copy(o, me, ctx_peer(o)).start()
    for o in range(1, n_dp):
        gb_copy(o, me, lane, dp_peer(o)).start()
    for o in range(1, n_ctx):
        c = ctx_peer(o)
        ga_copy(o, c, me).wait_recv()
        for k in range(1, n_dp):
            gb_copy(k, c, lane, dp_peer(k)).start()
    for k in range(1, n_dp):
        for c in range(n_ctx):
            gb_copy(k, c, dp_peer(k), lane).wait_recv()
    st_copy(ticks - 1).wait_recv()

    for t in range(ticks):
        st_copy(t).wait_send()
        for o in range(1, n_ctx):
            peer = ctx_peer(o)
            kv_copy(t, o, me, peer).wait_send()
            nt_copy(t, o, me, peer).wait_send()
            kt_copy(t, o, me, peer).wait_send()
            gr_copy(t, o, me, peer).wait_send()
    for o in range(1, n_dp):
        ws_copy(o, lane, dp_peer(o)).wait_send()
        for c in range(n_ctx):
            gb_copy(o, c, lane, dp_peer(o)).wait_send()
    for o in range(1, n_ctx):
        ga_copy(o, me, ctx_peer(o)).wait_send()


def shards(sizes, state, weights, out_grad, start_span, block_order):
    n_pipe, n_ctx, n_dp = sizes
    rows, feat = state.shape[2:]
    spans, cols = weights.shape[0], weights.shape[3]
    hd = cols // 2
    stack = (feat // hd) * rows
    ticks = out_grad.shape[0]
    half_len = rows * n_ctx // block_order.shape[0]
    f_ctx = feat // n_ctx
    f_dp = f_ctx // n_dp
    cfg = (n_pipe, n_ctx, n_dp, ticks, half_len)
    dma = pltpu.SemaphoreType.DMA
    vmem = pl.BlockSpec(memory_space=pltpu.VMEM)
    smem = pl.BlockSpec(memory_space=pltpu.SMEM)
    new_state, gathered = pl.pallas_call(
        functools.partial(kernel, cfg),
        out_shape=(
            jax.ShapeDtypeStruct((rows, feat), BF16),
            jax.ShapeDtypeStruct((n_ctx, n_dp, spans, f_dp, cols), BF16),
        ),
        in_specs=[vmem, vmem, vmem, smem, smem],
        out_specs=(vmem, vmem),
        scratch_shapes=[
            pltpu.VMEM((ticks, n_ctx, rows, cols), BF16),
            pltpu.VMEM((stack, hd), BF16),
            pltpu.VMEM((stack, hd), BF16),
            pltpu.VMEM((hd, stack), BF16),
            pltpu.VMEM((n_ctx, rows, stack), BF16),
            pltpu.VMEM((hd, stack), F32),
            pltpu.VMEM((1, stack), F32),
            pltpu.VMEM((1, stack), F32),
            pltpu.VMEM((ticks, rows, hd), F32),
            pltpu.VMEM((ticks, rows, feat), BF16),
            pltpu.VMEM((ticks, rows, feat), BF16),
            pltpu.VMEM((ticks, feat, rows), BF16),
            pltpu.VMEM((ticks, n_ctx, f_ctx, rows), BF16),
            pltpu.VMEM((ticks, n_ctx, rows, cols), BF16),
            pltpu.VMEM((ticks, n_ctx, rows, cols), BF16),
            pltpu.VMEM((ticks, rows, cols), BF16),
            pltpu.VMEM((ticks, n_ctx, rows, cols), BF16),
            pltpu.VMEM((ticks, f_ctx, cols), F32),
            pltpu.VMEM((n_dp, spans, f_dp, cols), BF16),
            pltpu.VMEM((n_dp, spans, f_dp, cols), BF16),
        ]
        + [dma((ticks, n_ctx))] * 8
        + [dma((ticks,))] * 2
        + [dma((n_dp,))] * 2
        + [dma((n_ctx,))] * 2
        + [dma((n_dp, n_ctx)), dma((n_ctx, n_dp))],
        compiler_params=pltpu.CompilerParams(
            collective_id=0, has_side_effects=True, vmem_limit_bytes=48 * 1024 * 1024
        ),
        name="window",
    )(state[0, 0], weights[:, 0], out_grad[:, 0, 0], start_span, block_order)
    grads = gathered.transpose(2, 0, 1, 3, 4).reshape(spans, feat, cols).astype(F32)
    return (new_state[None, None], grads[:, None])


def solution(mesh):
    sizes = (mesh.shape["pipe"], mesh.shape["ctx"], mesh.shape["dp"])
    return jax.shard_map(
        functools.partial(shards, sizes),
        mesh=mesh,
        in_specs=(
            P("pipe", "dp", "ctx", None),
            P(None, "pipe", None, None),
            P(None, "pipe", "dp", "ctx", None),
            P(None, "dp"),
            P(),
        ),
        out_specs=(P("pipe", "dp", "ctx", None), P(None, "pipe", None, None)),
        check_vma=False,
    )
```

```python
import functools
import math

import jax
import jax.numpy as jnp
from jax import lax
from jax.experimental import pallas as pl
from jax.experimental.pallas import tpu as pltpu
from jax.sharding import PartitionSpec as P

EPS = 1e-05
F32 = jnp.float32
BF16 = jnp.bfloat16
MESH = pl.DeviceIdType.MESH


def dot(a, b):
    return jnp.dot(a, b, preferred_element_type=F32)


def dot_nt(a, b):
    return lax.dot_general(a, b, (((1,), (1,)), ((), ())), preferred_element_type=F32)


def steps(count, body):
    if count <= 4:
        for index in range(count):
            body(index)
    else:
        lax.fori_loop(0, count, lambda index, none: (body(index), none)[1], None)


def kernel(
    cfg,
    state_hbm,
    weights_hbm,
    upstream_hbm,
    span_ref,
    order_ref,
    state_out,
    gathered,
    state_ref,
    weights_ref,
    upstream_ref,
    load_sem,
    kv,
    queries,
    up_rows,
    up_cols,
    exps,
    out_cols,
    totals,
    deltas,
    key_raw,
    updated,
    arrived,
    normed_t,
    normed_in,
    terms_out,
    terms_in,
    term_own,
    grad_rows,
    slices,
    wsend,
    wrecv,
    kv_send,
    kv_recv,
    nt_send,
    nt_recv,
    kt_send,
    kt_recv,
    gr_send,
    gr_recv,
    st_send,
    st_recv,
    ws_send,
    ws_recv,
    ga_send,
    ga_recv,
    gb_send,
    gb_recv,
):
    n_pipe, n_ctx, n_dp, ticks, half_len = cfg
    rows, feat = state_ref.shape
    hd = weights_ref.shape[2] // 2
    heads = feat // hd
    stack = heads * rows
    width = min(stack, 2 * rows)
    chunks = [slice(i * width, (i + 1) * width) for i in range(stack // width)]
    per_dev = rows // half_len
    f_ctx = feat // n_ctx
    f_dp = f_ctx // n_dp
    score_scale = 1.0 / math.sqrt(hd)
    exp_scale = score_scale * math.log2(math.e)

    sec = lax.axis_index("pipe")
    me = lax.axis_index("ctx")
    lane = lax.axis_index("dp")
    behind = lax.rem(sec + n_pipe - 1, n_pipe)
    ahead = lax.rem(sec + 1, n_pipe)

    def ctx_peer(offset):
        return lax.rem(me + offset, n_ctx)

    def dp_peer(offset):
        return lax.rem(lane + offset, n_dp)

    loads = [
        pltpu.make_async_copy(src, dst, load_sem.at[i])
        for i, (src, dst) in enumerate(
            [(state_hbm, state_ref), (weights_hbm, weights_ref), (upstream_hbm, upstream_ref)]
        )
    ]
    for load in loads:
        load.start()
    barrier = pltpu.get_barrier_semaphore()

    def greet(axis, who):
        pl.semaphore_signal(barrier, inc=1, device_id={axis: who}, device_id_type=MESH)

    for o in range(1, n_ctx):
        greet("ctx", ctx_peer(o))
    for o in range(1, n_dp):
        greet("dp", dp_peer(o))
    greet("pipe", behind)
    greet("pipe", ahead)

    def remote(src, dst, send, recv, axis, who):
        return pltpu.make_async_remote_copy(
            src_ref=src,
            dst_ref=dst,
            send_sem=send,
            recv_sem=recv,
            device_id={axis: who},
            device_id_type=MESH,
        )

    def kv_copy(t, o, owner, to):
        return remote(
            kv.at[t, owner], kv.at[t, owner], kv_send.at[t, o], kv_recv.at[t, owner], "ctx", to
        )

    def nt_copy(t, o, frm, to):
        return remote(
            normed_t.at[t, pl.ds(pl.multiple_of(to * f_ctx, 16), f_ctx)],
            normed_in.at[t, frm],
            nt_send.at[t, o],
            nt_recv.at[t, frm],
            "ctx",
            to,
        )

    def kt_copy(t, o, frm, to):
        return remote(
            terms_out.at[t, to],
            terms_in.at[t, frm],
            kt_send.at[t, o],
            kt_recv.at[t, frm],
            "ctx",
            to,
        )

    def gr_copy(t, o, owner, to):
        return remote(
            grad_rows.at[t, owner],
            grad_rows.at[t, owner],
            gr_send.at[t, o],
            gr_recv.at[t, owner],
            "ctx",
            to,
        )

    def st_copy(t):
        dst = state_out if t == ticks - 1 else arrived.at[t]
        return remote(updated.at[t], dst, st_send.at[t], st_recv.at[t], "pipe", ahead)

    def ws_copy(o, frm, to):
        return remote(wsend.at[to], wrecv.at[frm], ws_send.at[o], ws_recv.at[frm], "dp", to)

    def ga_copy(o, owner, to):
        return remote(
            gathered.at[owner, lane],
            gathered.at[owner, lane],
            ga_send.at[o],
            ga_recv.at[owner],
            "ctx",
            to,
        )

    def gb_copy(o, c, owner, to):
        return remote(
            gathered.at[c, owner],
            gathered.at[c, owner],
            gb_send.at[o, c],
            gb_recv.at[c, owner],
            "dp",
            to,
        )

    def positions(which, shape, axis):
        row = lax.rem(lax.broadcasted_iota(jnp.int32, shape, axis), rows)
        part = row // half_len
        base = jnp.zeros(shape, jnp.int32)
        for i in range(per_dev):
            base = jnp.where(part == i, order_ref[which * per_dev + i], base)
        return base * half_len + lax.rem(row, half_len)

    own_pos = positions(me, (1, width), 1)

    def span_at(t):
        anchor = lax.rem(sec - t + n_pipe * ticks, n_pipe)
        return lax.rem(span_ref[anchor] + (anchor + t) // n_pipe, 2)

    def begin(t, source):
        if t == 0:
            loads[0].wait()
        x = source[...].astype(F32)
        squares = x * x
        sums = [
            jnp.sum(squares[:, h * hd : (h + 1) * hd], axis=1, keepdims=True) for h in range(heads)
        ]
        scale = lax.rsqrt(sum(sums[1:], sums[0]) * (1.0 / feat) + EPS)
        normed = (x * scale).astype(BF16)
        if t == 0:
            loads[1].wait()
        projected = dot(normed, weights_ref[span_at(t)])
        raw = projected[:, :hd]
        key_raw[t] = raw
        key_unit = raw * lax.rsqrt(jnp.mean(raw * raw, axis=1, keepdims=True) + EPS)
        kv[t, me] = jnp.concatenate([key_unit, projected[:, hd:]], axis=1).astype(BF16)
        if t == 0:
            pl.semaphore_wait(barrier, n_ctx + n_dp)
        for o in range(1, n_ctx):
            kv_copy(t, o, me, ctx_peer(o)).start()
        if t == 0:
            loads[2].wait()
        for h in range(heads):
            part = x[:, h * hd : (h + 1) * hd]
            queries[h * rows : (h + 1) * rows, :] = (
                part * lax.rsqrt(sums[h] * (1.0 / hd) + EPS)
            ).astype(BF16)
            normed_t[t, h * hd : (h + 1) * hd, :] = (part * scale).T.astype(BF16)
            up = upstream_ref[t, :, h * hd : (h + 1) * hd]
            up_rows[h * rows : (h + 1) * rows, :] = up
            up_cols[:, h * rows : (h + 1) * rows] = up.astype(F32).T.astype(BF16)
        for o in range(1, n_ctx):
            nt_copy(t, o, me, ctx_peer(o)).start()

    def attend(t, block, first):
        keys = kv[t, block, :, :hd]
        values_t = kv[t, block, :, hd:].astype(F32).T.astype(BF16)
        causal = positions(block, (rows, 1), 0) <= own_pos
        for cut in chunks:
            scores = dot_nt(keys, queries[cut, :])
            weight = jnp.where(causal, jnp.exp2(scores * exp_scale), 0.0)
            total = jnp.sum(weight, axis=0, keepdims=True)
            rounded = weight.astype(BF16)
            exps[block, :, cut] = rounded
            mixed = dot(values_t, rounded)
            if first:
                totals[:, cut] = total
                out_cols[:, cut] = mixed
            else:
                totals[:, cut] += total
                out_cols[:, cut] += mixed

    def update(t, source):
        inverse = 1.0 / totals[...]
        totals[...] = inverse
        power = jnp.zeros((1, rows), F32)
        for h in range(heads):
            cut = slice(h * rows, (h + 1) * rows)
            part = out_cols[:, cut] * inverse[:, cut]
            out_cols[:, cut] = part
            deltas[:, cut] = jnp.sum(part * up_cols[:, cut].astype(F32), axis=0, keepdims=True)
            power = power + jnp.sum(part * part, axis=0, keepdims=True)
        scale = lax.rsqrt(power * (1.0 / feat) + EPS)
        for h in range(heads):
            cut = slice(h * hd, (h + 1) * hd)
            part = (out_cols[:, h * rows : (h + 1) * rows] * scale).T
            updated[t, :, cut] = (source[:, cut].astype(F32) + part).astype(BF16)
        st_copy(t).start()

    def backward(t, block):
        values = kv[t, block, :, hd:]
        key_grad = jnp.zeros((rows, hd), F32)
        value_grad = jnp.zeros((rows, hd), F32)
        for cut in chunks:
            probs = exps[block, :, cut].astype(F32) * totals[:, cut]
            prob_grad = dot(values, up_cols[:, cut])
            score_grad = (probs * (prob_grad - deltas[:, cut])).astype(BF16)
            value_grad = value_grad + dot(probs.astype(BF16), up_rows[cut, :])
            key_grad = key_grad + dot(score_grad, queries[cut, :])
        return jnp.concatenate([key_grad * score_scale, value_grad], axis=1).astype(BF16)

    def finish_rows(t):
        sums = term_own[t].astype(F32)
        for o in range(1, n_ctx):
            peer = ctx_peer(o)
            kt_copy(t, o, peer, me).wait_recv()
            sums = sums + terms_in[t, peer].astype(F32)
        raw = key_raw[t]
        scale = lax.rsqrt(jnp.mean(raw * raw, axis=1, keepdims=True) + EPS)
        unit = raw * scale
        delta = sums[:, :hd]
        back = scale * (delta - unit * jnp.mean(delta * unit, axis=1, keepdims=True))
        grad_rows[t, me] = jnp.concatenate([back, sums[:, hd:]], axis=1).astype(BF16)
        for o in range(1, n_ctx):
            gr_copy(t, o, me, ctx_peer(o)).start()

    def weight_slice(t):
        own = normed_t[t, pl.ds(pl.multiple_of(me * f_ctx, 16), f_ctx), :]
        total = dot(own, grad_rows[t, me])
        for o in range(1, n_ctx):
            peer = ctx_peer(o)
            nt_copy(t, o, peer, me).wait_recv()
            gr_copy(t, o, peer, me).wait_recv()
            total = total + dot(normed_in[t, peer], grad_rows[t, peer])
        return total

    for t in range(ticks):
        if t == 0:
            source = state_ref
        else:
            st_copy(t - 1).wait_recv()
            source = arrived.at[t - 1]
        begin(t, source)
        attend(t, me, True)
        if t > 0:
            finish_rows(t - 1)

        def later(index, t=t):
            peer = ctx_peer(index + 1)
            kv_copy(t, 0, peer, me).wait_recv()
            attend(t, peer, False)

        steps(n_ctx - 1, later)
        update(t, source)

        def give(index, t=t):
            peer = ctx_peer(index + 1)
            terms_out[t, peer] = backward(t, peer)
            kt_copy(t, index + 1, me, peer).start()

        steps(n_ctx - 1, give)
        term_own[t] = backward(t, me)

    for t in range(ticks - 1):
        slices[t] = weight_slice(t)
    finish_rows(ticks - 1)
    slices[ticks - 1] = weight_slice(ticks - 1)
    picked = [span_at(t).astype(F32) for t in range(ticks)]
    for d in range(n_dp):
        cut = slice(d * f_dp, (d + 1) * f_dp)
        parts = [slices[t, cut, :] for t in range(ticks)]
        high = sum(part * pick for part, pick in zip(parts, picked))
        low = sum(part * (1.0 - pick) for part, pick in zip(parts, picked))
        wsend[d, 0] = low.astype(BF16)
        wsend[d, 1] = high.astype(BF16)
    for o in range(1, n_dp):
        ws_copy(o, lane, dp_peer(o)).start()
    total = wsend[lane].astype(F32)
    for o in range(1, n_dp):
        peer = dp_peer(o)
        ws_copy(o, peer, lane).wait_recv()
        total = total + wrecv[peer].astype(F32)
    gathered[me, lane] = total.astype(BF16)
    for o in range(1, n_ctx):
        ga_copy(o, me, ctx_peer(o)).start()
    near = lane + 1 - 2 * lax.rem(lane, 2)
    hops = n_dp // 2

    def pair(index):
        return lax.rem(lane + 2 * index, n_dp)

    order = [ctx_peer(o) for o in range(n_ctx)]
    for o, c in enumerate(order):
        if o:
            ga_copy(o, c, me).wait_recv()
        for k in range(1, hops):
            gb_copy(k, c, lane, pair(k)).start()
        gb_copy(0, c, lane, near).start()
    for c in order:
        for k in range(1, hops):
            gb_copy(k, c, pair(k), lane).wait_recv()
            gb_copy(hops + k - 1, c, pair(k), near).start()
    for c in order:
        gb_copy(0, c, near, lane).wait_recv()
        for k in range(1, hops):
            gb_copy(0, c, lax.rem(near + 2 * k, n_dp), lane).wait_recv()
    st_copy(ticks - 1).wait_recv()

    for t in range(ticks):
        st_copy(t).wait_send()
        for o in range(1, n_ctx):
            peer = ctx_peer(o)
            kv_copy(t, o, me, peer).wait_send()
            nt_copy(t, o, me, peer).wait_send()
            kt_copy(t, o, me, peer).wait_send()
            gr_copy(t, o, me, peer).wait_send()
    for o in range(1, n_dp):
        ws_copy(o, lane, dp_peer(o)).wait_send()
    for c in range(n_ctx):
        for k in range(2 * hops - 1):
            gb_copy(k, c, lane, near).wait_send()
    for o in range(1, n_ctx):
        ga_copy(o, me, ctx_peer(o)).wait_send()


def shards(sizes, state, weights, out_grad, start_span, block_order):
    n_pipe, n_ctx, n_dp = sizes
    rows, feat = state.shape[2:]
    spans, cols = weights.shape[0], weights.shape[3]
    hd = cols // 2
    stack = (feat // hd) * rows
    ticks = out_grad.shape[0]
    half_len = rows * n_ctx // block_order.shape[0]
    f_ctx = feat // n_ctx
    f_dp = f_ctx // n_dp
    cfg = (n_pipe, n_ctx, n_dp, ticks, half_len)
    dma = pltpu.SemaphoreType.DMA
    vmem = pl.BlockSpec(memory_space=pltpu.VMEM)
    hbm = pl.BlockSpec(memory_space=pltpu.HBM)
    smem = pl.BlockSpec(memory_space=pltpu.SMEM)
    new_state, gathered = pl.pallas_call(
        functools.partial(kernel, cfg),
        out_shape=(
            jax.ShapeDtypeStruct((rows, feat), BF16),
            jax.ShapeDtypeStruct((n_ctx, n_dp, spans, f_dp, cols), BF16),
        ),
        in_specs=[hbm, hbm, hbm, smem, smem],
        out_specs=(vmem, vmem),
        scratch_shapes=[
            pltpu.VMEM((rows, feat), BF16),
            pltpu.VMEM((spans, feat, cols), BF16),
            pltpu.VMEM((ticks, rows, feat), BF16),
            dma((3,)),
            pltpu.VMEM((ticks, n_ctx, rows, cols), BF16),
            pltpu.VMEM((stack, hd), BF16),
            pltpu.VMEM((stack, hd), BF16),
            pltpu.VMEM((hd, stack), BF16),
            pltpu.VMEM((n_ctx, rows, stack), BF16),
            pltpu.VMEM((hd, stack), F32),
            pltpu.VMEM((1, stack), F32),
            pltpu.VMEM((1, stack), F32),
            pltpu.VMEM((ticks, rows, hd), F32),
            pltpu.VMEM((ticks, rows, feat), BF16),
            pltpu.VMEM((ticks, rows, feat), BF16),
            pltpu.VMEM((ticks, feat, rows), BF16),
            pltpu.VMEM((ticks, n_ctx, f_ctx, rows), BF16),
            pltpu.VMEM((ticks, n_ctx, rows, cols), BF16),
            pltpu.VMEM((ticks, n_ctx, rows, cols), BF16),
            pltpu.VMEM((ticks, rows, cols), BF16),
            pltpu.VMEM((ticks, n_ctx, rows, cols), BF16),
            pltpu.VMEM((ticks, f_ctx, cols), F32),
            pltpu.VMEM((n_dp, spans, f_dp, cols), BF16),
            pltpu.VMEM((n_dp, spans, f_dp, cols), BF16),
        ]
        + [dma((ticks, n_ctx))] * 8
        + [dma((ticks,))] * 2
        + [dma((n_dp,))] * 2
        + [dma((n_ctx,))] * 2
        + [dma((n_dp, n_ctx)), dma((n_ctx, n_dp))],
        compiler_params=pltpu.CompilerParams(
            collective_id=0, has_side_effects=True, vmem_limit_bytes=60 * 1024 * 1024
        ),
        name="window",
    )(state[0, 0], weights[:, 0], out_grad[:, 0, 0], start_span[:, 0], block_order)
    grads = gathered.transpose(2, 0, 1, 3, 4).reshape(spans, feat, cols).astype(F32)
    return (new_state[None, None], grads[:, None])


def solution(mesh):
    sizes = (mesh.shape["pipe"], mesh.shape["ctx"], mesh.shape["dp"])
    return jax.shard_map(
        functools.partial(shards, sizes),
        mesh=mesh,
        in_specs=(
            P("pipe", "dp", "ctx", None),
            P(None, "pipe", None, None),
            P(None, "pipe", "dp", "ctx", None),
            P(None, "dp"),
            P(),
        ),
        out_specs=(P("pipe", "dp", "ctx", None), P(None, "pipe", None, None)),
        check_vma=False,
    )
```

```python
import functools
import math

import jax
import jax.numpy as jnp
from jax import lax
from jax.experimental import pallas as pl
from jax.experimental.pallas import tpu as pltpu
from jax.sharding import PartitionSpec as P

EPS = 1e-05
F32 = jnp.float32
BF16 = jnp.bfloat16
MESH = pl.DeviceIdType.MESH


def dot(a, b):
    return jnp.dot(a, b, preferred_element_type=F32)


def dot_nt(a, b):
    return lax.dot_general(a, b, (((1,), (1,)), ((), ())), preferred_element_type=F32)


def steps(count, body):
    if count <= 4:
        for index in range(count):
            body(index)
    else:
        lax.fori_loop(0, count, lambda index, none: (body(index), none)[1], None)


def kernel(
    cfg,
    state_hbm,
    weights_hbm,
    upstream_hbm,
    span_ref,
    order_ref,
    state_out,
    gathered,
    state_ref,
    weights_ref,
    upstream_ref,
    load_sem,
    kv,
    queries,
    up_rows,
    up_cols,
    exps,
    out_cols,
    totals,
    deltas,
    key_raw,
    updated,
    arrived,
    normed_t,
    normed_in,
    terms_out,
    terms_in,
    term_own,
    grad_rows,
    slices,
    wsend,
    wrecv,
    kv_send,
    kv_recv,
    nt_send,
    nt_recv,
    kt_send,
    kt_recv,
    gr_send,
    gr_recv,
    st_send,
    st_recv,
    ws_send,
    ws_recv,
    ga_send,
    ga_recv,
    gb_send,
    gb_recv,
):
    n_pipe, n_ctx, n_dp, ticks, half_len = cfg
    rows, feat = state_ref.shape
    hd = weights_ref.shape[2] // 2
    heads = feat // hd
    stack = heads * rows
    width = min(stack, 2 * rows)
    chunks = [slice(i * width, (i + 1) * width) for i in range(stack // width)]
    per_dev = rows // half_len
    f_ctx = feat // n_ctx
    f_dp = f_ctx // n_dp
    score_scale = 1.0 / math.sqrt(hd)
    exp_scale = score_scale * math.log2(math.e)

    sec = lax.axis_index("pipe")
    me = lax.axis_index("ctx")
    lane = lax.axis_index("dp")
    behind = lax.rem(sec + n_pipe - 1, n_pipe)
    ahead = lax.rem(sec + 1, n_pipe)

    def ctx_peer(offset):
        return lax.rem(me + offset, n_ctx)

    def dp_peer(offset):
        return lax.rem(lane + offset, n_dp)

    loads = [
        pltpu.make_async_copy(src, dst, load_sem.at[i])
        for i, (src, dst) in enumerate(
            [(state_hbm, state_ref), (weights_hbm, weights_ref), (upstream_hbm, upstream_ref)]
        )
    ]
    for load in loads:
        load.start()
    def beside(side):
        return lax.rem(me + 2 * side - 1 + n_ctx, n_ctx)

    def exists(side):
        return me > 0 if side == 0 else me < n_ctx - 1

    def from_line(index, act):
        distance = index + 1

        @pl.when(me - distance >= 0)
        def _():
            act(me - distance, 1)

        @pl.when(me + distance < n_ctx)
        def _():
            act(me + distance, 0)

    def spread(copy):
        for side in (0, 1):

            @pl.when(exists(side))
            def _(side=side):
                copy(me, side).start()

    def take(copy, owner, side):
        copy(owner, side).wait_recv()

        @pl.when(exists(side))
        def _():
            copy(owner, side).start()

    def drain(copy):
        def sent(owner, side):
            @pl.when(exists(side))
            def _():
                copy(owner, side).wait_send()

        for side in (0, 1):
            sent(me, side)
        steps(n_ctx - 1, lambda index: from_line(index, sent))

    barrier = pltpu.get_barrier_semaphore()

    def greet(axis, who):
        pl.semaphore_signal(barrier, inc=1, device_id={axis: who}, device_id_type=MESH)

    for o in range(1, n_ctx):
        greet("ctx", ctx_peer(o))
    for o in range(1, n_dp):
        greet("dp", dp_peer(o))
    greet("pipe", behind)
    greet("pipe", ahead)

    def remote(src, dst, send, recv, axis, who):
        return pltpu.make_async_remote_copy(
            src_ref=src,
            dst_ref=dst,
            send_sem=send,
            recv_sem=recv,
            device_id={axis: who},
            device_id_type=MESH,
        )

    def kv_copy(t, owner, side):
        block = kv.at[t, owner]
        return remote(
            block, block, kv_send.at[t, owner, side], kv_recv.at[t, owner], "ctx", beside(side)
        )

    def nt_copy(t, o, frm, to):
        return remote(
            normed_t.at[t, pl.ds(pl.multiple_of(to * f_ctx, 16), f_ctx)],
            normed_in.at[t, frm],
            nt_send.at[t, o],
            nt_recv.at[t, frm],
            "ctx",
            to,
        )

    def kt_copy(t, o, frm, to):
        return remote(
            terms_out.at[t, to],
            terms_in.at[t, frm],
            kt_send.at[t, o],
            kt_recv.at[t, frm],
            "ctx",
            to,
        )

    def gr_copy(t, owner, side):
        block = grad_rows.at[t, owner]
        return remote(
            block, block, gr_send.at[t, owner, side], gr_recv.at[t, owner], "ctx", beside(side)
        )

    def st_copy(t):
        dst = state_out if t == ticks - 1 else arrived.at[t]
        return remote(updated.at[t], dst, st_send.at[t], st_recv.at[t], "pipe", ahead)

    def ws_copy(o, frm, to):
        return remote(wsend.at[to], wrecv.at[frm], ws_send.at[o], ws_recv.at[frm], "dp", to)

    def piece(c, d):
        first = pl.multiple_of((c * n_dp + d) * f_dp, f_dp)
        return gathered.at[:, pl.ds(first, f_dp), :]

    def ga_copy(owner, side):
        block = piece(owner, lane)
        return remote(
            block, block, ga_send.at[owner, side], ga_recv.at[owner], "ctx", beside(side)
        )

    def gb_copy(o, c, owner, to):
        return remote(
            piece(c, owner),
            piece(c, owner),
            gb_send.at[o, c],
            gb_recv.at[c, owner],
            "dp",
            to,
        )

    def positions(which, shape, axis):
        row = lax.rem(lax.broadcasted_iota(jnp.int32, shape, axis), rows)
        part = row // half_len
        base = jnp.zeros(shape, jnp.int32)
        for i in range(per_dev):
            base = jnp.where(part == i, order_ref[which * per_dev + i], base)
        return base * half_len + lax.rem(row, half_len)

    own_pos = positions(me, (1, width), 1)

    def span_at(t):
        anchor = lax.rem(sec - t + n_pipe * ticks, n_pipe)
        return lax.rem(span_ref[anchor] + (anchor + t) // n_pipe, 2)

    def begin(t, source):
        if t == 0:
            loads[0].wait()
        x = source[...].astype(F32)
        squares = x * x
        sums = [
            jnp.sum(squares[:, h * hd : (h + 1) * hd], axis=1, keepdims=True) for h in range(heads)
        ]
        scale = lax.rsqrt(sum(sums[1:], sums[0]) * (1.0 / feat) + EPS)
        normed = (x * scale).astype(BF16)
        if t == 0:
            loads[1].wait()
        projected = dot(normed, weights_ref[span_at(t)])
        raw = projected[:, :hd]
        key_raw[t] = raw
        key_unit = raw * lax.rsqrt(jnp.mean(raw * raw, axis=1, keepdims=True) + EPS)
        kv[t, me] = jnp.concatenate([key_unit, projected[:, hd:]], axis=1).astype(BF16)
        if t == 0:
            pl.semaphore_wait(barrier, n_ctx + n_dp)
        spread(functools.partial(kv_copy, t))
        if t == 0:
            loads[2].wait()
        for h in range(heads):
            part = x[:, h * hd : (h + 1) * hd]
            queries[h * rows : (h + 1) * rows, :] = (
                part * lax.rsqrt(sums[h] * (1.0 / hd) + EPS)
            ).astype(BF16)
            normed_t[t, h * hd : (h + 1) * hd, :] = (part * scale).T.astype(BF16)
            up = upstream_ref[t, :, h * hd : (h + 1) * hd]
            up_rows[h * rows : (h + 1) * rows, :] = up
            up_cols[:, h * rows : (h + 1) * rows] = up.astype(F32).T.astype(BF16)

    def attend(t, block, first):
        keys = kv[t, block, :, :hd]
        values_t = kv[t, block, :, hd:].astype(F32).T.astype(BF16)
        causal = positions(block, (rows, 1), 0) <= own_pos
        for cut in chunks:
            scores = dot_nt(keys, queries[cut, :])
            weight = jnp.where(causal, jnp.exp2(scores * exp_scale), 0.0)
            total = jnp.sum(weight, axis=0, keepdims=True)
            rounded = weight.astype(BF16)
            exps[block, :, cut] = rounded
            mixed = dot(values_t, rounded)
            if first:
                totals[:, cut] = total
                out_cols[:, cut] = mixed
            else:
                totals[:, cut] += total
                out_cols[:, cut] += mixed

    def update(t, source):
        inverse = 1.0 / totals[...]
        totals[...] = inverse
        power = jnp.zeros((1, rows), F32)
        for h in range(heads):
            cut = slice(h * rows, (h + 1) * rows)
            part = out_cols[:, cut] * inverse[:, cut]
            out_cols[:, cut] = part
            deltas[:, cut] = jnp.sum(part * up_cols[:, cut].astype(F32), axis=0, keepdims=True)
            power = power + jnp.sum(part * part, axis=0, keepdims=True)
        scale = lax.rsqrt(power * (1.0 / feat) + EPS)
        for h in range(heads):
            cut = slice(h * hd, (h + 1) * hd)
            part = (out_cols[:, h * rows : (h + 1) * rows] * scale).T
            updated[t, :, cut] = (source[:, cut].astype(F32) + part).astype(BF16)
        st_copy(t).start()

    def backward(t, block):
        values = kv[t, block, :, hd:]
        key_grad = jnp.zeros((rows, hd), F32)
        value_grad = jnp.zeros((rows, hd), F32)
        for cut in chunks:
            probs = exps[block, :, cut].astype(F32) * totals[:, cut]
            prob_grad = dot(values, up_cols[:, cut])
            score_grad = (probs * (prob_grad - deltas[:, cut])).astype(BF16)
            value_grad = value_grad + dot(probs.astype(BF16), up_rows[cut, :])
            key_grad = key_grad + dot(score_grad, queries[cut, :])
        return jnp.concatenate([key_grad * score_scale, value_grad], axis=1).astype(BF16)

    def finish_rows(t):
        sums = term_own[t].astype(F32)
        for o in range(1, n_ctx):
            peer = ctx_peer(o)
            kt_copy(t, o, peer, me).wait_recv()
            sums = sums + terms_in[t, peer].astype(F32)
        raw = key_raw[t]
        scale = lax.rsqrt(jnp.mean(raw * raw, axis=1, keepdims=True) + EPS)
        unit = raw * scale
        delta = sums[:, :hd]
        back = scale * (delta - unit * jnp.mean(delta * unit, axis=1, keepdims=True))
        grad_rows[t, me] = jnp.concatenate([back, sums[:, hd:]], axis=1).astype(BF16)
        spread(functools.partial(gr_copy, t))

    def weight_slice(t):
        own = normed_t[t, pl.ds(pl.multiple_of(me * f_ctx, 16), f_ctx), :]
        slices[t] = dot(own, grad_rows[t, me])
        for o in range(1, n_ctx):
            nt_copy(t, o, ctx_peer(o), me).wait_recv()

        def add(owner, side):
            take(functools.partial(gr_copy, t), owner, side)
            slices[t] += dot(normed_in[t, owner], grad_rows[t, owner])

        steps(n_ctx - 1, lambda index: from_line(index, add))

    for t in range(ticks):
        if t == 0:
            source = state_ref
        else:
            st_copy(t - 1).wait_recv()
            source = arrived.at[t - 1]
        begin(t, source)
        attend(t, me, True)
        if t > 0:
            finish_rows(t - 1)

        def later(owner, side, t=t):
            take(functools.partial(kv_copy, t), owner, side)
            attend(t, owner, False)

        steps(n_ctx - 1, lambda index, later=later: from_line(index, later))
        for o in range(1, n_ctx):
            nt_copy(t, o, me, ctx_peer(o)).start()
        update(t, source)

        def give(index, t=t):
            peer = ctx_peer(index + 1)
            terms_out[t, peer] = backward(t, peer)
            kt_copy(t, index + 1, me, peer).start()

        steps(n_ctx - 1, give)
        term_own[t] = backward(t, me)

    for t in range(ticks - 1):
        weight_slice(t)
    finish_rows(ticks - 1)
    weight_slice(ticks - 1)
    picked = [span_at(t).astype(F32) for t in range(ticks)]
    for d in range(n_dp):
        cut = slice(d * f_dp, (d + 1) * f_dp)
        parts = [slices[t, cut, :] for t in range(ticks)]
        high = sum(part * pick for part, pick in zip(parts, picked))
        low = sum(part * (1.0 - pick) for part, pick in zip(parts, picked))
        wsend[d, 0] = low.astype(BF16)
        wsend[d, 1] = high.astype(BF16)
    for o in range(1, n_dp):
        ws_copy(o, lane, dp_peer(o)).start()
    total = wsend[lane].astype(F32)
    for o in range(1, n_dp):
        peer = dp_peer(o)
        ws_copy(o, peer, lane).wait_recv()
        total = total + wrecv[peer].astype(F32)
    gathered[:, pl.ds(pl.multiple_of((me * n_dp + lane) * f_dp, f_dp), f_dp), :] = total.astype(BF16)
    spread(ga_copy)
    near = lane + 1 - 2 * lax.rem(lane, 2)
    hops = n_dp // 2

    def pair(index):
        return lax.rem(lane + 2 * index, n_dp)

    def across(c):
        for k in range(1, hops):
            gb_copy(k, c, lane, pair(k)).start()
        gb_copy(0, c, lane, near).start()

    def onward(c):
        for k in range(1, hops):
            gb_copy(k, c, pair(k), lane).wait_recv()
            gb_copy(hops + k - 1, c, pair(k), near).start()

    def reach(owner, side):
        take(ga_copy, owner, side)
        across(owner)

    across(me)
    steps(n_ctx - 1, lambda index: from_line(index, reach))
    onward(me)
    steps(n_ctx - 1, lambda index: from_line(index, lambda owner, side: onward(owner)))
    for c in range(n_ctx):
        gb_copy(0, c, near, lane).wait_recv()
        for k in range(1, hops):
            gb_copy(0, c, lax.rem(near + 2 * k, n_dp), lane).wait_recv()
    st_copy(ticks - 1).wait_recv()

    for t in range(ticks):
        st_copy(t).wait_send()
        drain(functools.partial(kv_copy, t))
        drain(functools.partial(gr_copy, t))
        for o in range(1, n_ctx):
            peer = ctx_peer(o)
            nt_copy(t, o, me, peer).wait_send()
            kt_copy(t, o, me, peer).wait_send()
    for o in range(1, n_dp):
        ws_copy(o, lane, dp_peer(o)).wait_send()
    for c in range(n_ctx):
        for k in range(2 * hops - 1):
            gb_copy(k, c, lane, near).wait_send()
    drain(ga_copy)


def shards(sizes, state, weights, out_grad, start_span, block_order):
    n_pipe, n_ctx, n_dp = sizes
    rows, feat = state.shape[2:]
    spans, cols = weights.shape[0], weights.shape[3]
    hd = cols // 2
    stack = (feat // hd) * rows
    ticks = out_grad.shape[0]
    half_len = rows * n_ctx // block_order.shape[0]
    f_ctx = feat // n_ctx
    f_dp = f_ctx // n_dp
    cfg = (n_pipe, n_ctx, n_dp, ticks, half_len)
    dma = pltpu.SemaphoreType.DMA
    vmem = pl.BlockSpec(memory_space=pltpu.VMEM)
    hbm = pl.BlockSpec(memory_space=pltpu.HBM)
    smem = pl.BlockSpec(memory_space=pltpu.SMEM)
    new_state, gathered = pl.pallas_call(
        functools.partial(kernel, cfg),
        out_shape=(
            jax.ShapeDtypeStruct((rows, feat), BF16),
            jax.ShapeDtypeStruct((spans, feat, cols), BF16),
        ),
        in_specs=[hbm, hbm, hbm, smem, smem],
        out_specs=(vmem, vmem),
        scratch_shapes=[
            pltpu.VMEM((rows, feat), BF16),
            pltpu.VMEM((spans, feat, cols), BF16),
            pltpu.VMEM((ticks, rows, feat), BF16),
            dma((3,)),
            pltpu.VMEM((ticks, n_ctx, rows, cols), BF16),
            pltpu.VMEM((stack, hd), BF16),
            pltpu.VMEM((stack, hd), BF16),
            pltpu.VMEM((hd, stack), BF16),
            pltpu.VMEM((n_ctx, rows, stack), BF16),
            pltpu.VMEM((hd, stack), F32),
            pltpu.VMEM((1, stack), F32),
            pltpu.VMEM((1, stack), F32),
            pltpu.VMEM((ticks, rows, hd), F32),
            pltpu.VMEM((ticks, rows, feat), BF16),
            pltpu.VMEM((ticks, rows, feat), BF16),
            pltpu.VMEM((ticks, feat, rows), BF16),
            pltpu.VMEM((ticks, n_ctx, f_ctx, rows), BF16),
            pltpu.VMEM((ticks, n_ctx, rows, cols), BF16),
            pltpu.VMEM((ticks, n_ctx, rows, cols), BF16),
            pltpu.VMEM((ticks, rows, cols), BF16),
            pltpu.VMEM((ticks, n_ctx, rows, cols), BF16),
            pltpu.VMEM((ticks, f_ctx, cols), F32),
            pltpu.VMEM((n_dp, spans, f_dp, cols), BF16),
            pltpu.VMEM((n_dp, spans, f_dp, cols), BF16),
        ]
        + [dma((ticks, n_ctx, 2)), dma((ticks, n_ctx))]
        + [dma((ticks, n_ctx))] * 4
        + [dma((ticks, n_ctx, 2)), dma((ticks, n_ctx))]
        + [dma((ticks,))] * 2
        + [dma((n_dp,))] * 2
        + [dma((n_ctx, 2)), dma((n_ctx,))]
        + [dma((n_dp, n_ctx)), dma((n_ctx, n_dp))],
        compiler_params=pltpu.CompilerParams(
            collective_id=0, has_side_effects=True, vmem_limit_bytes=60 * 1024 * 1024
        ),
        name="window",
    )(state[0, 0], weights[:, 0], out_grad[:, 0, 0], start_span[:, 0], block_order)
    return (new_state[None, None], gathered.astype(F32)[:, None])


def solution(mesh):
    sizes = (mesh.shape["pipe"], mesh.shape["ctx"], mesh.shape["dp"])
    return jax.shard_map(
        functools.partial(shards, sizes),
        mesh=mesh,
        in_specs=(
            P("pipe", "dp", "ctx", None),
            P(None, "pipe", None, None),
            P(None, "pipe", "dp", "ctx", None),
            P(None, "dp"),
            P(),
        ),
        out_specs=(P("pipe", "dp", "ctx", None), P(None, "pipe", None, None)),
        check_vma=False,
    )
```

```python
import functools
import math

import jax
import jax.numpy as jnp
from jax import lax
from jax.experimental import pallas as pl
from jax.experimental.pallas import tpu as pltpu
from jax.sharding import PartitionSpec as P

EPS = 1e-05
F32 = jnp.float32
BF16 = jnp.bfloat16
MESH = pl.DeviceIdType.MESH


def dot(a, b):
    return jnp.dot(a, b, preferred_element_type=F32)


def dot_nt(a, b):
    return lax.dot_general(a, b, (((1,), (1,)), ((), ())), preferred_element_type=F32)


def steps(count, body):
    if count <= 4:
        for index in range(count):
            body(index)
    else:
        lax.fori_loop(0, count, lambda index, none: (body(index), none)[1], None)


def kernel(
    cfg,
    state_hbm,
    weights_hbm,
    upstream_hbm,
    span_ref,
    order_ref,
    state_out,
    gathered,
    state_ref,
    weights_ref,
    upstream_ref,
    load_sem,
    kv,
    queries,
    up_rows,
    up_cols,
    exps,
    out_cols,
    totals,
    deltas,
    key_raw,
    updated,
    arrived,
    normed_t,
    normed_in,
    terms_out,
    terms_in,
    term_own,
    grad_rows,
    slices,
    wsend,
    wrecv,
    kv_send,
    kv_recv,
    nt_send,
    nt_recv,
    kt_send,
    kt_recv,
    gr_send,
    gr_recv,
    st_send,
    st_recv,
    ws_send,
    ws_recv,
    ga_send,
    ga_recv,
    gb_send,
    gb_recv,
):
    n_pipe, n_ctx, n_dp, ticks, half_len = cfg
    rows, feat = state_ref.shape
    hd = weights_ref.shape[2] // 2
    heads = feat // hd
    stack = heads * rows
    width = min(stack, 2 * rows)
    chunks = [slice(i * width, (i + 1) * width) for i in range(stack // width)]
    per_dev = rows // half_len
    f_ctx = feat // n_ctx
    f_dp = f_ctx // n_dp
    score_scale = 1.0 / math.sqrt(hd)
    exp_scale = score_scale * math.log2(math.e)

    sec = lax.axis_index("pipe")
    me = lax.axis_index("ctx")
    lane = lax.axis_index("dp")
    behind = lax.rem(sec + n_pipe - 1, n_pipe)
    ahead = lax.rem(sec + 1, n_pipe)

    def ctx_peer(offset):
        return lax.rem(me + offset, n_ctx)

    def dp_peer(offset):
        return lax.rem(lane + offset, n_dp)

    loads = [
        pltpu.make_async_copy(src, dst, load_sem.at[i])
        for i, (src, dst) in enumerate(
            [(state_hbm, state_ref), (weights_hbm, weights_ref), (upstream_hbm, upstream_ref)]
        )
    ]
    for load in loads:
        load.start()
    barrier = pltpu.get_barrier_semaphore()

    def greet(axis, who):
        pl.semaphore_signal(barrier, inc=1, device_id={axis: who}, device_id_type=MESH)

    for o in range(1, n_ctx):
        greet("ctx", ctx_peer(o))
    for o in range(1, n_dp):
        greet("dp", dp_peer(o))
    greet("pipe", behind)
    greet("pipe", ahead)

    def remote(src, dst, send, recv, axis, who):
        return pltpu.make_async_remote_copy(
            src_ref=src,
            dst_ref=dst,
            send_sem=send,
            recv_sem=recv,
            device_id={axis: who},
            device_id_type=MESH,
        )

    def kv_copy(t, o, owner, to):
        return remote(
            kv.at[t, owner], kv.at[t, owner], kv_send.at[t, o], kv_recv.at[t, owner], "ctx", to
        )

    def nt_copy(t, o, frm, to):
        return remote(
            normed_t.at[t, pl.ds(pl.multiple_of(to * f_ctx, 16), f_ctx)],
            normed_in.at[t, frm],
            nt_send.at[t, o],
            nt_recv.at[t, frm],
            "ctx",
            to,
        )

    def kt_copy(t, o, frm, to):
        return remote(
            terms_out.at[t, to],
            terms_in.at[t, frm],
            kt_send.at[t, o],
            kt_recv.at[t, frm],
            "ctx",
            to,
        )

    def gr_copy(t, o, owner, to):
        return remote(
            grad_rows.at[t, owner],
            grad_rows.at[t, owner],
            gr_send.at[t, o],
            gr_recv.at[t, owner],
            "ctx",
            to,
        )

    def st_copy(t):
        dst = state_out if t == ticks - 1 else arrived.at[t]
        return remote(updated.at[t], dst, st_send.at[t], st_recv.at[t], "pipe", ahead)

    def ws_copy(o, frm, to):
        return remote(wsend.at[to], wrecv.at[frm], ws_send.at[o], ws_recv.at[frm], "dp", to)

    def ga_copy(o, owner, to):
        return remote(
            gathered.at[owner, lane],
            gathered.at[owner, lane],
            ga_send.at[o],
            ga_recv.at[owner],
            "ctx",
            to,
        )

    def gb_copy(o, c, owner, to):
        return remote(
            gathered.at[c, owner],
            gathered.at[c, owner],
            gb_send.at[o, c],
            gb_recv.at[c, owner],
            "dp",
            to,
        )

    def positions(which, shape, axis):
        row = lax.rem(lax.broadcasted_iota(jnp.int32, shape, axis), rows)
        part = row // half_len
        base = jnp.zeros(shape, jnp.int32)
        for i in range(per_dev):
            base = jnp.where(part == i, order_ref[which * per_dev + i], base)
        return base * half_len + lax.rem(row, half_len)

    own_pos = positions(me, (1, width), 1)

    def span_at(t):
        anchor = lax.rem(sec - t + n_pipe * ticks, n_pipe)
        return lax.rem(span_ref[anchor] + (anchor + t) // n_pipe, 2)

    def begin(t, source):
        if t == 0:
            loads[0].wait()
        x = source[...].astype(F32)
        squares = x * x
        sums = [
            jnp.sum(squares[:, h * hd : (h + 1) * hd], axis=1, keepdims=True) for h in range(heads)
        ]
        scale = lax.rsqrt(sum(sums[1:], sums[0]) * (1.0 / feat) + EPS)
        normed = (x * scale).astype(BF16)
        if t == 0:
            loads[1].wait()
        projected = dot(normed, weights_ref[span_at(t)])
        raw = projected[:, :hd]
        key_raw[t] = raw
        key_unit = raw * lax.rsqrt(jnp.mean(raw * raw, axis=1, keepdims=True) + EPS)
        kv[t, me] = jnp.concatenate([key_unit, projected[:, hd:]], axis=1).astype(BF16)
        if t == 0:
            pl.semaphore_wait(barrier, n_ctx + n_dp)
        for o in range(1, n_ctx):
            kv_copy(t, o, me, ctx_peer(o)).start()
        if t == 0:
            loads[2].wait()
        for h in range(heads):
            part = x[:, h * hd : (h + 1) * hd]
            queries[h * rows : (h + 1) * rows, :] = (
                part * lax.rsqrt(sums[h] * (1.0 / hd) + EPS)
            ).astype(BF16)
            normed_t[t, h * hd : (h + 1) * hd, :] = (part * scale).T.astype(BF16)
            up = upstream_ref[t, :, h * hd : (h + 1) * hd]
            up_rows[h * rows : (h + 1) * rows, :] = up
            up_cols[:, h * rows : (h + 1) * rows] = up.astype(F32).T.astype(BF16)
        for o in range(1, n_ctx):
            nt_copy(t, o, me, ctx_peer(o)).start()

    def attend(t, block, first):
        keys = kv[t, block, :, :hd]
        values_t = kv[t, block, :, hd:].astype(F32).T.astype(BF16)
        causal = positions(block, (rows, 1), 0) <= own_pos
        for cut in chunks:
            scores = dot_nt(keys, queries[cut, :])
            weight = jnp.where(causal, jnp.exp2(scores * exp_scale), 0.0)
            total = jnp.sum(weight, axis=0, keepdims=True)
            rounded = weight.astype(BF16)
            exps[block, :, cut] = rounded
            mixed = dot(values_t, rounded)
            if first:
                totals[:, cut] = total
                out_cols[:, cut] = mixed
            else:
                totals[:, cut] += total
                out_cols[:, cut] += mixed

    def normalise():
        inverse = 1.0 / totals[...]
        totals[...] = inverse
        for h in range(heads):
            cut = slice(h * rows, (h + 1) * rows)
            part = out_cols[:, cut] * inverse[:, cut]
            out_cols[:, cut] = part
            deltas[:, cut] = jnp.sum(part * up_cols[:, cut].astype(F32), axis=0, keepdims=True)

    def update(t, source):
        power = jnp.zeros((1, rows), F32)
        for h in range(heads):
            part = out_cols[:, h * rows : (h + 1) * rows]
            power = power + jnp.sum(part * part, axis=0, keepdims=True)
        scale = lax.rsqrt(power * (1.0 / feat) + EPS)
        for h in range(heads):
            cut = slice(h * hd, (h + 1) * hd)
            part = (out_cols[:, h * rows : (h + 1) * rows] * scale).T
            updated[t, :, cut] = (source[:, cut].astype(F32) + part).astype(BF16)
        st_copy(t).start()

    def backward(t, block):
        values = kv[t, block, :, hd:]
        key_grad = jnp.zeros((rows, hd), F32)
        value_grad = jnp.zeros((rows, hd), F32)
        for cut in chunks:
            probs = exps[block, :, cut].astype(F32) * totals[:, cut]
            prob_grad = dot(values, up_cols[:, cut])
            score_grad = (probs * (prob_grad - deltas[:, cut])).astype(BF16)
            value_grad = value_grad + dot(probs.astype(BF16), up_rows[cut, :])
            key_grad = key_grad + dot(score_grad, queries[cut, :])
        return jnp.concatenate([key_grad * score_scale, value_grad], axis=1).astype(BF16)

    def finish_rows(t):
        sums = term_own[t].astype(F32)
        for o in range(1, n_ctx):
            peer = ctx_peer(o)
            kt_copy(t, o, peer, me).wait_recv()
            sums = sums + terms_in[t, peer].astype(F32)
        raw = key_raw[t]
        scale = lax.rsqrt(jnp.mean(raw * raw, axis=1, keepdims=True) + EPS)
        unit = raw * scale
        delta = sums[:, :hd]
        back = scale * (delta - unit * jnp.mean(delta * unit, axis=1, keepdims=True))
        grad_rows[t, me] = jnp.concatenate([back, sums[:, hd:]], axis=1).astype(BF16)
        for o in range(1, n_ctx):
            gr_copy(t, o, me, ctx_peer(o)).start()

    def weight_slice(t):
        own = normed_t[t, pl.ds(pl.multiple_of(me * f_ctx, 16), f_ctx), :]
        total = dot(own, grad_rows[t, me])
        for o in range(1, n_ctx):
            peer = ctx_peer(o)
            nt_copy(t, o, peer, me).wait_recv()
            gr_copy(t, o, peer, me).wait_recv()
            total = total + dot(normed_in[t, peer], grad_rows[t, peer])
        return total

    for t in range(ticks):
        if t == 0:
            source = state_ref
        else:
            st_copy(t - 1).wait_recv()
            source = arrived.at[t - 1]
        begin(t, source)
        attend(t, me, True)
        if t > 0:
            finish_rows(t - 1)

        def later(index, t=t):
            peer = ctx_peer(index + 1)
            kv_copy(t, 0, peer, me).wait_recv()
            attend(t, peer, False)

        steps(n_ctx - 1, later)
        normalise()
        if t < ticks - 1:
            update(t, source)

        def give(index, t=t):
            peer = ctx_peer(index + 1)
            terms_out[t, peer] = backward(t, peer)
            kt_copy(t, index + 1, me, peer).start()

        steps(n_ctx - 1, give)
        term_own[t] = backward(t, me)
        if t == ticks - 1:
            update(t, source)

    for t in range(ticks - 1):
        slices[t] = weight_slice(t)
    finish_rows(ticks - 1)
    slices[ticks - 1] = weight_slice(ticks - 1)
    picked = [span_at(t).astype(F32) for t in range(ticks)]
    for d in range(n_dp):
        cut = slice(d * f_dp, (d + 1) * f_dp)
        parts = [slices[t, cut, :] for t in range(ticks)]
        high = sum(part * pick for part, pick in zip(parts, picked))
        low = sum(part * (1.0 - pick) for part, pick in zip(parts, picked))
        wsend[d, 0] = low.astype(BF16)
        wsend[d, 1] = high.astype(BF16)
    for o in range(1, n_dp):
        ws_copy(o, lane, dp_peer(o)).start()
    total = wsend[lane].astype(F32)
    for o in range(1, n_dp):
        peer = dp_peer(o)
        ws_copy(o, peer, lane).wait_recv()
        total = total + wrecv[peer].astype(F32)
    gathered[me, lane] = total.astype(BF16)
    for o in range(1, n_ctx):
        ga_copy(o, me, ctx_peer(o)).start()
    near = lane + 1 - 2 * lax.rem(lane, 2)
    hops = n_dp // 2

    def pair(index):
        return lax.rem(lane + 2 * index, n_dp)

    order = [ctx_peer(o) for o in range(n_ctx)]
    for o, c in enumerate(order):
        if o:
            ga_copy(o, c, me).wait_recv()
        for k in range(1, hops):
            gb_copy(k, c, lane, pair(k)).start()
        gb_copy(0, c, lane, near).start()
    for c in order:
        for k in range(1, hops):
            gb_copy(k, c, pair(k), lane).wait_recv()
            gb_copy(hops + k - 1, c, pair(k), near).start()
    for c in order:
        gb_copy(0, c, near, lane).wait_recv()
        for k in range(1, hops):
            gb_copy(0, c, lax.rem(near + 2 * k, n_dp), lane).wait_recv()
    st_copy(ticks - 1).wait_recv()

    for t in range(ticks):
        st_copy(t).wait_send()
        for o in range(1, n_ctx):
            peer = ctx_peer(o)
            kv_copy(t, o, me, peer).wait_send()
            nt_copy(t, o, me, peer).wait_send()
            kt_copy(t, o, me, peer).wait_send()
            gr_copy(t, o, me, peer).wait_send()
    for o in range(1, n_dp):
        ws_copy(o, lane, dp_peer(o)).wait_send()
    for c in range(n_ctx):
        for k in range(2 * hops - 1):
            gb_copy(k, c, lane, near).wait_send()
    for o in range(1, n_ctx):
        ga_copy(o, me, ctx_peer(o)).wait_send()


def shards(sizes, state, weights, out_grad, start_span, block_order):
    n_pipe, n_ctx, n_dp = sizes
    rows, feat = state.shape[2:]
    spans, cols = weights.shape[0], weights.shape[3]
    hd = cols // 2
    stack = (feat // hd) * rows
    ticks = out_grad.shape[0]
    half_len = rows * n_ctx // block_order.shape[0]
    f_ctx = feat // n_ctx
    f_dp = f_ctx // n_dp
    cfg = (n_pipe, n_ctx, n_dp, ticks, half_len)
    dma = pltpu.SemaphoreType.DMA
    vmem = pl.BlockSpec(memory_space=pltpu.VMEM)
    hbm = pl.BlockSpec(memory_space=pltpu.HBM)
    smem = pl.BlockSpec(memory_space=pltpu.SMEM)
    new_state, gathered = pl.pallas_call(
        functools.partial(kernel, cfg),
        out_shape=(
            jax.ShapeDtypeStruct((rows, feat), BF16),
            jax.ShapeDtypeStruct((n_ctx, n_dp, spans, f_dp, cols), BF16),
        ),
        in_specs=[hbm, hbm, hbm, smem, smem],
        out_specs=(vmem, vmem),
        scratch_shapes=[
            pltpu.VMEM((rows, feat), BF16),
            pltpu.VMEM((spans, feat, cols), BF16),
            pltpu.VMEM((ticks, rows, feat), BF16),
            dma((3,)),
            pltpu.VMEM((ticks, n_ctx, rows, cols), BF16),
            pltpu.VMEM((stack, hd), BF16),
            pltpu.VMEM((stack, hd), BF16),
            pltpu.VMEM((hd, stack), BF16),
            pltpu.VMEM((n_ctx, rows, stack), BF16),
            pltpu.VMEM((hd, stack), F32),
            pltpu.VMEM((1, stack), F32),
            pltpu.VMEM((1, stack), F32),
            pltpu.VMEM((ticks, rows, hd), F32),
            pltpu.VMEM((ticks, rows, feat), BF16),
            pltpu.VMEM((ticks, rows, feat), BF16),
            pltpu.VMEM((ticks, feat, rows), BF16),
            pltpu.VMEM((ticks, n_ctx, f_ctx, rows), BF16),
            pltpu.VMEM((ticks, n_ctx, rows, cols), BF16),
            pltpu.VMEM((ticks, n_ctx, rows, cols), BF16),
            pltpu.VMEM((ticks, rows, cols), BF16),
            pltpu.VMEM((ticks, n_ctx, rows, cols), BF16),
            pltpu.VMEM((ticks, f_ctx, cols), F32),
            pltpu.VMEM((n_dp, spans, f_dp, cols), BF16),
            pltpu.VMEM((n_dp, spans, f_dp, cols), BF16),
        ]
        + [dma((ticks, n_ctx))] * 8
        + [dma((ticks,))] * 2
        + [dma((n_dp,))] * 2
        + [dma((n_ctx,))] * 2
        + [dma((n_dp, n_ctx)), dma((n_ctx, n_dp))],
        compiler_params=pltpu.CompilerParams(
            collective_id=0, has_side_effects=True, vmem_limit_bytes=60 * 1024 * 1024
        ),
        name="window",
    )(state[0, 0], weights[:, 0], out_grad[:, 0, 0], start_span[:, 0], block_order)
    grads = gathered.transpose(2, 0, 1, 3, 4).reshape(spans, feat, cols).astype(F32)
    return (new_state[None, None], grads[:, None])


def solution(mesh):
    sizes = (mesh.shape["pipe"], mesh.shape["ctx"], mesh.shape["dp"])
    return jax.shard_map(
        functools.partial(shards, sizes),
        mesh=mesh,
        in_specs=(
            P("pipe", "dp", "ctx", None),
            P(None, "pipe", None, None),
            P(None, "pipe", "dp", "ctx", None),
            P(None, "dp"),
            P(),
        ),
        out_specs=(P("pipe", "dp", "ctx", None), P(None, "pipe", None, None)),
        check_vma=False,
    )
```

```python
import functools
import math

import jax
import jax.numpy as jnp
from jax import lax
from jax.experimental import pallas as pl
from jax.experimental.pallas import tpu as pltpu
from jax.sharding import PartitionSpec as P

EPS = 1e-05
F32 = jnp.float32
BF16 = jnp.bfloat16
MESH = pl.DeviceIdType.MESH


def dot(a, b):
    return jnp.dot(a, b, preferred_element_type=F32)


def dot_nt(a, b):
    return lax.dot_general(a, b, (((1,), (1,)), ((), ())), preferred_element_type=F32)


def steps(count, body):
    if count <= 4:
        for index in range(count):
            body(index)
    else:
        lax.fori_loop(0, count, lambda index, none: (body(index), none)[1], None)


def kernel(
    cfg,
    state_hbm,
    weights_hbm,
    upstream_hbm,
    span_ref,
    order_ref,
    state_out,
    gathered,
    state_ref,
    weights_ref,
    upstream_ref,
    load_sem,
    kv,
    queries,
    up_rows,
    up_cols,
    exps,
    out_cols,
    totals,
    deltas,
    key_raw,
    updated,
    arrived,
    normed_t,
    normed_in,
    terms_out,
    terms_in,
    term_own,
    grad_rows,
    slices,
    wsend,
    wrecv,
    kv_send,
    kv_recv,
    nt_send,
    nt_recv,
    kt_send,
    kt_recv,
    gr_send,
    gr_recv,
    st_send,
    st_recv,
    ws_send,
    ws_recv,
    ga_send,
    ga_recv,
    gb_send,
    gb_recv,
):
    n_pipe, n_ctx, n_dp, ticks, half_len = cfg
    rows, feat = state_ref.shape
    hd = weights_ref.shape[2] // 2
    heads = feat // hd
    stack = heads * rows
    width = min(stack, 2 * rows)
    chunks = [slice(i * width, (i + 1) * width) for i in range(stack // width)]
    per_dev = rows // half_len
    f_ctx = feat // n_ctx
    f_dp = f_ctx // n_dp
    score_scale = 1.0 / math.sqrt(hd)
    exp_scale = score_scale * math.log2(math.e)

    sec = lax.axis_index("pipe")
    me = lax.axis_index("ctx")
    lane = lax.axis_index("dp")
    behind = lax.rem(sec + n_pipe - 1, n_pipe)
    ahead = lax.rem(sec + 1, n_pipe)

    def ctx_peer(offset):
        return lax.rem(me + offset, n_ctx)

    def dp_peer(offset):
        return lax.rem(lane + offset, n_dp)

    loads = [
        pltpu.make_async_copy(src, dst, load_sem.at[i])
        for i, (src, dst) in enumerate(
            [(state_hbm, state_ref), (weights_hbm, weights_ref), (upstream_hbm, upstream_ref)]
        )
    ]
    for load in loads:
        load.start()
    barrier = pltpu.get_barrier_semaphore()

    def greet(axis, who):
        pl.semaphore_signal(barrier, inc=1, device_id={axis: who}, device_id_type=MESH)

    for o in range(1, n_ctx):
        greet("ctx", ctx_peer(o))
    for o in range(1, n_dp):
        greet("dp", dp_peer(o))
    greet("pipe", behind)
    greet("pipe", ahead)

    def remote(src, dst, send, recv, axis, who):
        return pltpu.make_async_remote_copy(
            src_ref=src,
            dst_ref=dst,
            send_sem=send,
            recv_sem=recv,
            device_id={axis: who},
            device_id_type=MESH,
        )

    def kv_copy(t, o, owner, to):
        return remote(
            kv.at[t, owner], kv.at[t, owner], kv_send.at[t, o], kv_recv.at[t, owner], "ctx", to
        )

    def nt_copy(t, o, frm, to):
        return remote(
            normed_t.at[t, pl.ds(pl.multiple_of(to * f_ctx, 16), f_ctx)],
            normed_in.at[t, frm],
            nt_send.at[t, o],
            nt_recv.at[t, frm],
            "ctx",
            to,
        )

    def kt_copy(t, o, frm, to):
        return remote(
            terms_out.at[t, to],
            terms_in.at[t, frm],
            kt_send.at[t, o],
            kt_recv.at[t, frm],
            "ctx",
            to,
        )

    def gr_copy(t, o, owner, to):
        return remote(
            grad_rows.at[t, owner],
            grad_rows.at[t, owner],
            gr_send.at[t, o],
            gr_recv.at[t, owner],
            "ctx",
            to,
        )

    def st_copy(t):
        dst = state_out if t == ticks - 1 else arrived.at[t]
        return remote(updated.at[t], dst, st_send.at[t], st_recv.at[t], "pipe", ahead)

    def ws_copy(o, frm, to):
        return remote(wsend.at[to], wrecv.at[frm], ws_send.at[o], ws_recv.at[frm], "dp", to)

    def ga_copy(o, owner, to):
        return remote(
            gathered.at[owner, lane],
            gathered.at[owner, lane],
            ga_send.at[o],
            ga_recv.at[owner],
            "ctx",
            to,
        )

    def gb_copy(o, c, owner, to):
        return remote(
            gathered.at[c, owner],
            gathered.at[c, owner],
            gb_send.at[o, c],
            gb_recv.at[c, owner],
            "dp",
            to,
        )

    def positions(which, shape, axis):
        row = lax.rem(lax.broadcasted_iota(jnp.int32, shape, axis), rows)
        part = row // half_len
        base = jnp.zeros(shape, jnp.int32)
        for i in range(per_dev):
            base = jnp.where(part == i, order_ref[which * per_dev + i], base)
        return base * half_len + lax.rem(row, half_len)

    own_pos = positions(me, (1, width), 1)

    def span_at(t):
        anchor = lax.rem(sec - t + n_pipe * ticks, n_pipe)
        return lax.rem(span_ref[anchor] + (anchor + t) // n_pipe, 2)

    def begin(t, source):
        if t == 0:
            loads[0].wait()
        x = source[...].astype(F32)
        squares = x * x
        sums = [
            jnp.sum(squares[:, h * hd : (h + 1) * hd], axis=1, keepdims=True) for h in range(heads)
        ]
        scale = lax.rsqrt(sum(sums[1:], sums[0]) * (1.0 / feat) + EPS)
        normed = (x * scale).astype(BF16)
        if t == 0:
            loads[1].wait()
        projected = dot(normed, weights_ref[span_at(t)])
        raw = projected[:, :hd]
        key_raw[t] = raw
        key_unit = raw * lax.rsqrt(jnp.mean(raw * raw, axis=1, keepdims=True) + EPS)
        kv[t, me] = jnp.concatenate([key_unit, projected[:, hd:]], axis=1).astype(BF16)
        if t == 0:
            pl.semaphore_wait(barrier, n_ctx + n_dp)
        for o in range(1, n_ctx):
            kv_copy(t, o, me, ctx_peer(o)).start()
        if t == 0:
            loads[2].wait()
        for h in range(heads):
            part = x[:, h * hd : (h + 1) * hd]
            queries[h * rows : (h + 1) * rows, :] = (
                part * lax.rsqrt(sums[h] * (1.0 / hd) + EPS)
            ).astype(BF16)
            normed_t[t, h * hd : (h + 1) * hd, :] = (part * scale).T.astype(BF16)
            up = upstream_ref[t, :, h * hd : (h + 1) * hd]
            up_rows[h * rows : (h + 1) * rows, :] = up
            up_cols[:, h * rows : (h + 1) * rows] = up.astype(F32).T.astype(BF16)

    def attend(t, block, first):
        keys = kv[t, block, :, :hd]
        values_t = kv[t, block, :, hd:].astype(F32).T.astype(BF16)
        causal = positions(block, (rows, 1), 0) <= own_pos
        for cut in chunks:
            scores = dot_nt(keys, queries[cut, :])
            weight = jnp.where(causal, jnp.exp2(scores * exp_scale), 0.0)
            total = jnp.sum(weight, axis=0, keepdims=True)
            rounded = weight.astype(BF16)
            exps[block, :, cut] = rounded
            mixed = dot(values_t, rounded)
            if first:
                totals[:, cut] = total
                out_cols[:, cut] = mixed
            else:
                totals[:, cut] += total
                out_cols[:, cut] += mixed

    def normalise():
        inverse = 1.0 / totals[...]
        totals[...] = inverse
        for h in range(heads):
            cut = slice(h * rows, (h + 1) * rows)
            part = out_cols[:, cut] * inverse[:, cut]
            out_cols[:, cut] = part
            deltas[:, cut] = jnp.sum(part * up_cols[:, cut].astype(F32), axis=0, keepdims=True)

    def update(t, source):
        power = jnp.zeros((1, rows), F32)
        for h in range(heads):
            part = out_cols[:, h * rows : (h + 1) * rows]
            power = power + jnp.sum(part * part, axis=0, keepdims=True)
        scale = lax.rsqrt(power * (1.0 / feat) + EPS)
        for h in range(heads):
            cut = slice(h * hd, (h + 1) * hd)
            part = (out_cols[:, h * rows : (h + 1) * rows] * scale).T
            updated[t, :, cut] = (source[:, cut].astype(F32) + part).astype(BF16)
        st_copy(t).start()

    def backward(t, block):
        values = kv[t, block, :, hd:]
        key_grad = jnp.zeros((rows, hd), F32)
        value_grad = jnp.zeros((rows, hd), F32)
        for cut in chunks:
            probs = exps[block, :, cut].astype(F32) * totals[:, cut]
            prob_grad = dot(values, up_cols[:, cut])
            score_grad = (probs * (prob_grad - deltas[:, cut])).astype(BF16)
            value_grad = value_grad + dot(probs.astype(BF16), up_rows[cut, :])
            key_grad = key_grad + dot(score_grad, queries[cut, :])
        return jnp.concatenate([key_grad * score_scale, value_grad], axis=1).astype(BF16)

    def finish_rows(t):
        sums = term_own[t].astype(F32)
        for o in range(1, n_ctx):
            peer = ctx_peer(o)
            kt_copy(t, o, peer, me).wait_recv()
            sums = sums + terms_in[t, peer].astype(F32)
        raw = key_raw[t]
        scale = lax.rsqrt(jnp.mean(raw * raw, axis=1, keepdims=True) + EPS)
        unit = raw * scale
        delta = sums[:, :hd]
        back = scale * (delta - unit * jnp.mean(delta * unit, axis=1, keepdims=True))
        grad_rows[t, me] = jnp.concatenate([back, sums[:, hd:]], axis=1).astype(BF16)
        for o in range(1, n_ctx):
            gr_copy(t, o, me, ctx_peer(o)).start()

    def weight_slice(t):
        own = normed_t[t, pl.ds(pl.multiple_of(me * f_ctx, 16), f_ctx), :]
        total = dot(own, grad_rows[t, me])
        for o in range(1, n_ctx):
            peer = ctx_peer(o)
            nt_copy(t, o, peer, me).wait_recv()
            gr_copy(t, o, peer, me).wait_recv()
            total = total + dot(normed_in[t, peer], grad_rows[t, peer])
        return total

    for t in range(ticks):
        if t == 0:
            source = state_ref
        else:
            st_copy(t - 1).wait_recv()
            source = arrived.at[t - 1]
        begin(t, source)
        attend(t, me, True)
        if t > 0:
            finish_rows(t - 1)

        def later(index, t=t):
            peer = ctx_peer(index + 1)
            kv_copy(t, 0, peer, me).wait_recv()
            attend(t, peer, False)

        steps(n_ctx - 1, later)
        normalise()
        if t < ticks - 1:
            update(t, source)

        def give(index, t=t):
            peer = ctx_peer(index + 1)
            terms_out[t, peer] = backward(t, peer)
            kt_copy(t, index + 1, me, peer).start()

        steps(n_ctx - 1, give)
        for o in range(1, n_ctx):
            nt_copy(t, o, me, ctx_peer(o)).start()
        term_own[t] = backward(t, me)
        if t == ticks - 1:
            update(t, source)

    for t in range(ticks - 1):
        slices[t] = weight_slice(t)
    finish_rows(ticks - 1)
    slices[ticks - 1] = weight_slice(ticks - 1)
    picked = [span_at(t).astype(F32) for t in range(ticks)]
    for d in range(n_dp):
        cut = slice(d * f_dp, (d + 1) * f_dp)
        parts = [slices[t, cut, :] for t in range(ticks)]
        high = sum(part * pick for part, pick in zip(parts, picked))
        low = sum(part * (1.0 - pick) for part, pick in zip(parts, picked))
        wsend[d, 0] = low.astype(BF16)
        wsend[d, 1] = high.astype(BF16)
    for o in range(1, n_dp):
        ws_copy(o, lane, dp_peer(o)).start()
    total = wsend[lane].astype(F32)
    for o in range(1, n_dp):
        peer = dp_peer(o)
        ws_copy(o, peer, lane).wait_recv()
        total = total + wrecv[peer].astype(F32)
    gathered[me, lane] = total.astype(BF16)
    for o in range(1, n_ctx):
        ga_copy(o, me, ctx_peer(o)).start()
    near = lane + 1 - 2 * lax.rem(lane, 2)
    hops = n_dp // 2

    def pair(index):
        return lax.rem(lane + 2 * index, n_dp)

    order = [ctx_peer(o) for o in range(n_ctx)]
    for o, c in enumerate(order):
        if o:
            ga_copy(o, c, me).wait_recv()
        for k in range(1, hops):
            gb_copy(k, c, lane, pair(k)).start()
        gb_copy(0, c, lane, near).start()
    for c in order:
        for k in range(1, hops):
            gb_copy(k, c, pair(k), lane).wait_recv()
            gb_copy(hops + k - 1, c, pair(k), near).start()
    for c in order:
        gb_copy(0, c, near, lane).wait_recv()
        for k in range(1, hops):
            gb_copy(0, c, lax.rem(near + 2 * k, n_dp), lane).wait_recv()
    st_copy(ticks - 1).wait_recv()

    for t in range(ticks):
        st_copy(t).wait_send()
        for o in range(1, n_ctx):
            peer = ctx_peer(o)
            kv_copy(t, o, me, peer).wait_send()
            nt_copy(t, o, me, peer).wait_send()
            kt_copy(t, o, me, peer).wait_send()
            gr_copy(t, o, me, peer).wait_send()
    for o in range(1, n_dp):
        ws_copy(o, lane, dp_peer(o)).wait_send()
    for c in range(n_ctx):
        for k in range(2 * hops - 1):
            gb_copy(k, c, lane, near).wait_send()
    for o in range(1, n_ctx):
        ga_copy(o, me, ctx_peer(o)).wait_send()


def shards(sizes, state, weights, out_grad, start_span, block_order):
    n_pipe, n_ctx, n_dp = sizes
    rows, feat = state.shape[2:]
    spans, cols = weights.shape[0], weights.shape[3]
    hd = cols // 2
    stack = (feat // hd) * rows
    ticks = out_grad.shape[0]
    half_len = rows * n_ctx // block_order.shape[0]
    f_ctx = feat // n_ctx
    f_dp = f_ctx // n_dp
    cfg = (n_pipe, n_ctx, n_dp, ticks, half_len)
    dma = pltpu.SemaphoreType.DMA
    vmem = pl.BlockSpec(memory_space=pltpu.VMEM)
    hbm = pl.BlockSpec(memory_space=pltpu.HBM)
    smem = pl.BlockSpec(memory_space=pltpu.SMEM)
    new_state, gathered = pl.pallas_call(
        functools.partial(kernel, cfg),
        out_shape=(
            jax.ShapeDtypeStruct((rows, feat), BF16),
            jax.ShapeDtypeStruct((n_ctx, n_dp, spans, f_dp, cols), BF16),
        ),
        in_specs=[hbm, hbm, hbm, smem, smem],
        out_specs=(vmem, vmem),
        scratch_shapes=[
            pltpu.VMEM((rows, feat), BF16),
            pltpu.VMEM((spans, feat, cols), BF16),
            pltpu.VMEM((ticks, rows, feat), BF16),
            dma((3,)),
            pltpu.VMEM((ticks, n_ctx, rows, cols), BF16),
            pltpu.VMEM((stack, hd), BF16),
            pltpu.VMEM((stack, hd), BF16),
            pltpu.VMEM((hd, stack), BF16),
            pltpu.VMEM((n_ctx, rows, stack), BF16),
            pltpu.VMEM((hd, stack), F32),
            pltpu.VMEM((1, stack), F32),
            pltpu.VMEM((1, stack), F32),
            pltpu.VMEM((ticks, rows, hd), F32),
            pltpu.VMEM((ticks, rows, feat), BF16),
            pltpu.VMEM((ticks, rows, feat), BF16),
            pltpu.VMEM((ticks, feat, rows), BF16),
            pltpu.VMEM((ticks, n_ctx, f_ctx, rows), BF16),
            pltpu.VMEM((ticks, n_ctx, rows, cols), BF16),
            pltpu.VMEM((ticks, n_ctx, rows, cols), BF16),
            pltpu.VMEM((ticks, rows, cols), BF16),
            pltpu.VMEM((ticks, n_ctx, rows, cols), BF16),
            pltpu.VMEM((ticks, f_ctx, cols), F32),
            pltpu.VMEM((n_dp, spans, f_dp, cols), BF16),
            pltpu.VMEM((n_dp, spans, f_dp, cols), BF16),
        ]
        + [dma((ticks, n_ctx))] * 8
        + [dma((ticks,))] * 2
        + [dma((n_dp,))] * 2
        + [dma((n_ctx,))] * 2
        + [dma((n_dp, n_ctx)), dma((n_ctx, n_dp))],
        compiler_params=pltpu.CompilerParams(
            collective_id=0, has_side_effects=True, vmem_limit_bytes=60 * 1024 * 1024
        ),
        name="window",
    )(state[0, 0], weights[:, 0], out_grad[:, 0, 0], start_span[:, 0], block_order)
    grads = gathered.transpose(2, 0, 1, 3, 4).reshape(spans, feat, cols).astype(F32)
    return (new_state[None, None], grads[:, None])


def solution(mesh):
    sizes = (mesh.shape["pipe"], mesh.shape["ctx"], mesh.shape["dp"])
    return jax.shard_map(
        functools.partial(shards, sizes),
        mesh=mesh,
        in_specs=(
            P("pipe", "dp", "ctx", None),
            P(None, "pipe", None, None),
            P(None, "pipe", "dp", "ctx", None),
            P(None, "dp"),
            P(),
        ),
        out_specs=(P("pipe", "dp", "ctx", None), P(None, "pipe", None, None)),
        check_vma=False,
    )
```
